32 devices in a mesh: occ: 8 (over y, x, core), grp: 4 (over z).
Axes of the slice: x: 2, y: 2, z: 4, core: 2. Of those that a mesh axis runs over, the one named last changes fastest.
Arguments:
- slabs: float32 [32, 512, 1024], P(('occ', 'grp')), may hold values from -1.2 to 1.2
- occ_energy: float32 [32], replicated, may hold values from -1.5 to -0.3
- vir_energy: float32 [512], replicated, may hold values from 0.1 to 3
- pair_mask: int32 [32, 2], replicated, may hold values from 0 to 1, as said below
Outputs:
- aux_grad: float32 [32, 512, 1024], P(('occ', 'grp'))
- vir_density: float32 [512, 512], P('occ')
The draws below stay inside these ranges and needn't reach their ends.
Inputs may be any that keep to these rules, and one draw needn't show every extreme that they name: Entries are 0 or 1; orbital 0 is paired with all of its 2 partners, and so is every orbital i >= 32 - 1 - 2 (pair_mask[i, k - 1] = 1 for every 1 <= k <= 2 on those rows).
All inputs are finite; a program needn't handle non-finite values.
Results may differ from the reference program's by a relative error of at most 0.0003.
Values sent between devices are 32-bit elements; how exact they have to be, the bound alone decides.
No kernel may reach another device: no remote copies, remote signals or barrier semaphores. Data moves between devices by JAX's collectives and lax.ppermute only.
A program may use at most 128 MiB of HBM per device.

```python
import jax
import jax.numpy as jnp
from jax import lax

V = 512
A = 1024
KOFF = 2
NOCC = 32


def draw_pair_mask(key, part):
    ticket = jax.random.randint(jax.random.fold_in(key, 17), (NOCC, KOFF), 0, 5)
    chosen = (ticket < 2).astype(jnp.int32)
    chosen = chosen.at[0].set(1)
    return chosen.at[NOCC - 1 - KOFF:].set(1)


def raised(values, stream_key, source, target, blocks, factor):
    owner, partner = [(jnp.arange(values.shape[position]) // (values.shape[position] // blocks)).reshape([-1 if axis == position else 1 for axis in range(values.ndim)]) for position in (source, target)]
    chosen = jax.random.permutation(stream_key, blocks)[partner]
    strong = (owner == chosen) | (owner == (partner + blocks // 2) % blocks)
    return jnp.where(strong, factor * values, values)


def block_levels(rng, shape, pieces, low, largest):
    loudness = 1.0
    for dim, parts in pieces:
        draws = jax.random.uniform(jax.random.fold_in(jax.random.fold_in(rng, 6), dim), (parts,), jnp.float32, low / len(pieces), largest / len(pieces))
        loudness = loudness * jnp.repeat(jnp.exp(draws), shape[dim] // parts).reshape((-1,) + (1,) * (len(shape) - 1 - dim))
    return loudness


def heavy_noise(own_key, dims, spread, most, split, heavy, kind=jnp.bfloat16):
    entries = spread * jax.random.normal(own_key, dims, jnp.float32)
    if split:
        entries = entries * block_levels(own_key, dims, split, -0.22, 0.18)
    return jnp.clip(raised(entries, jax.random.fold_in(own_key, 3), *heavy), -most, most).astype(kind)


def setup_inputs(seed: int = 0) -> dict:
    streams_of = jax.random.split(jax.random.key(seed), 5)
    return {
        "slabs": heavy_noise(streams_of[0], (NOCC, V, A), 0.15, 1.2, ((0, 32),), (0, 1, 32, 2.75), jnp.float32),
        "occ_energy": jnp.clip(jax.random.uniform(streams_of[1], (NOCC,), jnp.float32, -1.5, -0.3), -1.5, -0.3),
        "vir_energy": jnp.clip(jax.random.uniform(streams_of[2], (V,), jnp.float32, 0.1, 3.0), 0.1, 3.0),
        "pair_mask": draw_pair_mask(jax.random.fold_in(streams_of[4], 71), 0),
    }


highest = lax.Precision.HIGHEST


def pair_terms(left_slab, right_slab, left_energy, right_energy, virtual):
    coulomb = jnp.dot(left_slab, right_slab.T, precision=highest, preferred_element_type=jnp.float32)
    denominator = left_energy + right_energy - virtual[:, None] - virtual[None, :]
    amplitude = coulomb / denominator
    grad_left = jnp.dot(amplitude, right_slab, precision=highest, preferred_element_type=jnp.float32)
    grad_right = jnp.dot(amplitude.T, left_slab, precision=highest, preferred_element_type=jnp.float32)
    density = jnp.dot(amplitude, amplitude.T, precision=highest, preferred_element_type=jnp.float32)
    density = density + jnp.dot(amplitude.T, amplitude, precision=highest, preferred_element_type=jnp.float32)
    return grad_left, grad_right, density


def reference(slabs, occ_energy, vir_energy, pair_mask):
    orbitals = slabs.shape[0]

    def visit(state_pair, orbital):
        grads, density = state_pair
        own_slab = lax.dynamic_index_in_dim(slabs, orbital, 0, keepdims=False)
        own_energy = lax.dynamic_index_in_dim(occ_energy, orbital, 0, keepdims=False)
        grad_left, grad_right, term = pair_terms(own_slab, own_slab, own_energy, own_energy, vir_energy)
        grads = grads.at[orbital].add(grad_left + grad_right)
        density = density + term
        for offset in range(1, KOFF + 1):
            partner = orbital + offset
            clipped = jnp.minimum(partner, orbitals - 1).astype(jnp.int32)
            flag = lax.dynamic_index_in_dim(pair_mask[:, offset - 1], orbital, 0, keepdims=False)
            active = ((flag == 1) & (partner < orbitals)).astype(jnp.float32)
            partner_slab = lax.dynamic_index_in_dim(slabs, clipped, 0, keepdims=False)
            partner_energy = lax.dynamic_index_in_dim(occ_energy, clipped, 0, keepdims=False)
            grad_left, grad_right, term = pair_terms(own_slab, partner_slab, own_energy, partner_energy, vir_energy)
            grads = grads.at[orbital].add(active * grad_left)
            grads = grads.at[clipped].add(active * grad_right)
            density = density + active * term
        return (grads, density), None

    start_state = (jnp.zeros(slabs.shape, jnp.float32), jnp.zeros((slabs.shape[1], slabs.shape[1]), jnp.float32))
    order = jnp.arange(orbitals, dtype=jnp.int32)
    (grads, density), unused = lax.scan(visit, start_state, order)
    return grads, density / orbitals
```

```python
import jax
import jax.numpy as jnp
import numpy as np
from jax import lax
from jax.sharding import PartitionSpec as P

AXES = ("occ", "grp")
CHUNKS = 2


def plan(nocc, ngrp):
    total = nocc * ngrp
    swap = nocc % 4 == 0

    def host(orbital):
        block, place = divmod(orbital, ngrp)
        if swap and block % 2 == 1:
            block = (block + nocc // 2) % nocc
        return block * ngrp + place

    routes = {name: [] for name in ("home", "visit", "back", "far", "near", "result")}
    fields = ("own", "one", "two", "far", "near")
    index = {name: np.zeros(total, np.int32) for name in fields}
    valid = {name: np.zeros(total, np.int32) for name in fields}
    half = nocc // 2
    for orbital in range(total):
        block, place = divmod(orbital, ngrp)
        sign = 1 if block < half else -1
        role = place if sign == 1 else ngrp - 1 - place
        device = host(orbital)
        index["own"][device] = orbital
        valid["own"][device] = 1
        if device != orbital:
            routes["home"].append((orbital, device))
        if role + 1 < ngrp:
            index["one"][device], valid["one"][device] = orbital + sign, 1
            routes["visit"].append((host(orbital + sign), device))
            routes["back"].append((device, host(orbital + sign)))
            routes["result"].append((device, orbital + sign))
        if role + 2 < ngrp:
            index["two"][device], valid["two"][device] = orbital + 2 * sign, 1
        following = block + sign
        if 0 <= following < nocc and not (sign == -1 and block == half):
            first = following * ngrp + (0 if sign == 1 else ngrp - 1)
            if role == ngrp - 4:
                index["far"][device], valid["far"][device] = first, 1
                routes["far"].append((first, device))
            if role == ngrp - 3:
                index["far"][device], valid["far"][device] = first + sign, 1
                index["near"][device], valid["near"][device] = first, 1
                routes["far"].append((first + sign, device))
                routes["near"].append((first, device))
    return routes, index, valid


def flipped(route):
    return [(target, source) for source, target in route]


def move(block, route):
    return lax.ppermute(block, AXES, route)


def mul(left, right, dims):
    return lax.dot_general(
        left, right, (dims, ((), ())), precision=lax.Precision.HIGH, preferred_element_type=jnp.float32
    )


def product_rows(left, right):
    return mul(left, right, ((1,), (1,)))


def product(left, right):
    return mul(left, right, ((1,), (0,)))


def product_columns(left, right):
    return mul(left, right, ((0,), (0,)))


def body(slabs, occ_energy, vir_energy, pair_mask):
    nocc, ngrp = lax.axis_size("occ"), lax.axis_size("grp")
    routes, index, valid = plan(nocc, ngrp)
    device = lax.axis_index(AXES)
    home = slabs[0]
    rows = home.shape[0]
    step = rows // CHUNKS

    names = ("own", "one", "two", "far", "near")
    table = jnp.asarray(np.stack([index[n] for n in names] + [valid[n] for n in names], 1))
    mine = lax.dynamic_index_in_dim(table, device, 0, keepdims=False)
    where = dict(zip(names, mine[:5]))
    there = dict(zip(names, mine[5:]))
    energy = {n: occ_energy[where[n]] for n in names}
    energy["home"] = occ_energy[device]

    def active(x, y, offset, ok):
        flag = pair_mask[jnp.minimum(where[x], where[y]), offset - 1]
        return jnp.where((flag == 1) & (ok == 1), 1.0, 0.0).astype(jnp.float32)

    def weight(x, y, flag, part):
        lowered = energy[x] + energy[y] - vir_energy[:, None] - vir_energy[None, part]
        return flag / lowered

    everything = slice(0, rows)
    on_odd = where["own"] != device

    own_parts = []
    for c in range(CHUNKS):
        piece = home[c * step:(c + 1) * step]
        if routes["home"]:
            piece = jnp.where(on_odd, move(piece, routes["home"]), piece)
        own_parts.append(piece)
    one_parts = [move(piece, routes["visit"]) for piece in own_parts]
    two_parts = [move(piece, routes["visit"]) for piece in one_parts]
    far = move(home, routes["far"])
    near = move(home, routes["near"])
    own = jnp.concatenate(own_parts, 0)
    one = jnp.concatenate(one_parts, 0)

    t_home = product_rows(home, home) * weight("home", "home", 1.0, everything)
    gradient = 2.0 * product(t_home, home)
    density = 2.0 * product_rows(t_home, t_home)

    t_one = product_rows(own, one) * weight("own", "one", active("own", "one", 1, there["one"]), everything)
    grad_own = product(t_one, one)
    grad_one = product_columns(t_one, own)
    density = density + product_rows(t_one, t_one) + product_columns(t_one, t_one)

    flags = {
        "own": active("own", "two", 2, there["two"]),
        "far": active("two", "far", 2, there["far"]),
        "near": active("two", "near", 1, there["near"]),
    }
    still = {"own": own, "far": far, "near": near}
    back_parts, t_two = [], {n: [] for n in still}
    for c in range(CHUNKS):
        part = slice(c * step, (c + 1) * step)
        back = 0.0
        for n, slab in still.items():
            t = product_rows(slab, two_parts[c]) * weight(n, "two", flags[n], part)
            t_two[n].append(t)
            back = back + product_columns(t, slab)
        back_parts.append(move(back, routes["back"]))
    two = jnp.concatenate(two_parts, 0)
    t_two = {n: jnp.concatenate(parts, 1) for n, parts in t_two.items()}
    grad_own = grad_own + product(t_two["own"], two)
    grad_far = product(t_two["far"], two)
    grad_near = product(t_two["near"], two)
    for t in t_two.values():
        density = density + product_rows(t, t) + product_columns(t, t)

    result = [
        move(grad_one[c * step:(c + 1) * step] + back_parts[c], routes["result"]) for c in range(CHUNKS)
    ]
    gradient = gradient + move(grad_far, flipped(routes["far"])) + move(grad_near, flipped(routes["near"]))
    if routes["home"]:
        returned = move(grad_own, flipped(routes["home"]))
        gradient = gradient + jnp.where(on_odd, returned, grad_own)
    else:
        gradient = gradient + grad_own
    gradient = gradient + jnp.concatenate(result, 0)

    return gradient[None], reduced(density, nocc, ngrp) / (nocc * ngrp)


def reduced(density, nocc, ngrp):
    if nocc & (nocc - 1) or ngrp & (ngrp - 1):
        return lax.psum(lax.psum_scatter(density, "occ", scatter_dimension=0, tiled=True), "grp")
    place = lax.axis_index("occ")
    width = density.shape[1]
    rows = density.shape[0] // nocc
    bit = 1
    blocks = density
    while bit < nocc:
        blocks = blocks.reshape(-1, 2, rows, width)
        side = (place // bit) % 2
        keep = lax.dynamic_index_in_dim(blocks, side, 1, keepdims=False)
        give = lax.dynamic_index_in_dim(blocks, 1 - side, 1, keepdims=False)
        route = [(o, o ^ bit) for o in range(nocc)]
        blocks = keep + lax.ppermute(give, "occ", route)
        bit *= 2
    blocks = blocks.reshape(rows, width)
    bit = 1
    while bit < ngrp:
        blocks = blocks + lax.ppermute(blocks, "grp", [(g, g ^ bit) for g in range(ngrp)])
        bit *= 2
    return blocks


def solution(mesh):
    placed = (P(AXES, None, None), P(), P(), P())
    return jax.shard_map(
        body,
        mesh=mesh,
        in_specs=placed,
        out_specs=(P(AXES, None, None), P("occ", None)),
        check_vma=False,
    )
```

```python
import functools

import jax
import jax.numpy as jnp
from jax import lax
from jax.experimental import pallas as pl
from jax.experimental.pallas import tpu as pltpu
from jax.sharding import PartitionSpec as P

AXES = ("occ", "grp")
PIECES = 4
VMEM_LIMIT = 56 * 1024 * 1024

SMEM = pl.BlockSpec(memory_space=pltpu.SMEM)
VMEM = pl.BlockSpec(memory_space=pltpu.VMEM)
ANY = pl.BlockSpec(memory_space=pl.ANY)


def plan(nocc):
    names = ("early2", "late0", "early0", "late2", "early_p3", "to_early", "to_late", "early_home", "late_home", "before")
    routes = {name: [] for name in names}

    def both(name, source, target):
        routes[name].append(tuple(4 * block + place for block, place in (source, target)))
        routes[name].append(tuple(4 * (nocc - 1 - block) + 3 - place for block, place in (source, target)))

    for even in range(0, nocc, 2):
        odd = even + 1
        both("early2", (odd, 2), (odd, 1))
        both("late0", (even, 0), (even, 1))
        both("early0", (odd, 0), (odd, 1))
        both("late2", (even, 2), (even, 1))
        both("early_p3", (even, 3), (odd, 1))
        both("to_early", (even, 1), (odd, 1))
        both("to_late", (odd, 1), (even, 1))
        both("early_home", (odd, 1), (odd, 0))
        both("late_home", (even, 1), (even, 0))
        if even:
            both("before", (even - 1, 1), (even, 1))
    return routes


def move(block, route):
    return lax.ppermute(block, AXES, route)


def tied(x, *earlier):
    return lax.optimization_barrier((x, *earlier))[0]


class Place:
    def __init__(self, nocc, energy_ref, mask_ref):
        occ, grp = lax.axis_index("occ"), lax.axis_index("grp")
        self.energy_ref, self.mask_ref = energy_ref, mask_ref
        self.last = nocc * 4 - 1
        self.own = occ * 4 + grp
        self.lower = grp <= 1
        hub = (grp == 1) | (grp == 2)
        inner = (lax.rem(occ, 2) == 1) == self.lower
        self.early, self.late = hub & inner, hub & ~inner
        self.from_late, self.from_early = ~hub & ~inner, ~hub & inner
        step = jnp.where(self.lower, 1, -1)
        a0 = occ * 4 + jnp.where(self.lower, 0, 3)
        self.index = {"a0": a0, "a1": a0 + step, "a2": a0 + 2 * step, "a3": a0 + 3 * step, "p3": a0 - step, "p2": a0 - 2 * step}

    def pair(self, x, y):
        offset = {"a0a1": 1, "a0a2": 2, "a1a2": 1, "a1a3": 2, "a0p2": 2, "a0p3": 1, "a1p3": 2}[x + y]
        i, j = self.index[x], self.index[y]
        there = (j >= 0) & (j <= self.last)
        i, j = jnp.clip(i, 0, self.last), jnp.clip(j, 0, self.last)
        active = there & (self.mask_ref[jnp.minimum(i, j), offset - 1] == 1)
        return active, self.energy_ref[i] + self.energy_ref[j]


ROWS = ((1,), (1,))
PLAIN = ((1,), (0,))
COLUMNS = ((0,), (0,))


def mul(left, right, dims):
    return lax.dot_general(left, right, (dims, ((), ())), preferred_element_type=jnp.float32)


def halves(x):
    high = x.astype(jnp.bfloat16)
    return high, (x - high.astype(jnp.float32)).astype(jnp.bfloat16)


def parts(x, other, axis):
    high, low = halves(x)
    return jnp.concatenate([high, low, high] if other else [high, high, low], axis)


def half_squares(t):
    high, low = halves(t)
    left, right = [high, high], [high * 0.5, low]
    return mul(jnp.concatenate(left, 1), jnp.concatenate(right, 1), ROWS) + mul(
        jnp.concatenate(left, 0), jnp.concatenate(right, 0), COLUMNS
    )


def home_kernel(nocc, energy_ref, mask_ref, vir_ref, slab_ref, grad_ref, density_ref, levels_ref):
    rows = slab_ref.shape[0]
    spread = jnp.broadcast_to(vir_ref[...], (rows, rows))
    levels_ref[...] = spread + spread.T
    energy = energy_ref[Place(nocc, energy_ref, mask_ref).own]
    slab = slab_ref[...]
    t = mul(parts(slab, False, 1), parts(slab, True, 1), ROWS) / (2.0 * energy - levels_ref[...])
    t3 = parts(t, False, 1)
    grad_ref[...] = 2.0 * mul(t3, parts(slab, True, 0), PLAIN)
    density_ref[...] = mul(t3, parts(t, True, 1), ROWS)


def slots_of(tasks):
    found = {}
    for role, x, y, *_ in tasks:
        for orbital in (x, y):
            name = "own" if orbital == "a1" else role + orbital[1:] if orbital[0] == "a" else role + "_" + orbital
            if name not in found.setdefault(role, {}):
                found[role][name] = (len(found[role]), orbital)
    return found


def pairs_kernel(nocc, tasks, names, given, made, energy_ref, mask_ref, levels_ref, *refs):
    slabs, refs = dict(zip(names, refs[:len(names)])), refs[len(names):]
    before, refs = dict(zip(given, refs[:len(given)])), refs[len(given):]
    after, refs = dict(zip(made, refs[:len(made)])), refs[len(made):]
    slots, split, slabs_sem, sums, square, levels, t_ref, sums_sem, meta, energies, state = refs
    width = slots.shape[2]
    place = Place(nocc, energy_ref, mask_ref)
    roles = {"early": place.early, "late": place.late}
    layout = slots_of(tasks)
    needed = {role: [jnp.bool_(False)] * len(layout[role]) for role in layout}
    for k, (role, x, y, left, right, counted) in enumerate(tasks):
        active, energy = place.pair(x, y)
        active = active & roles[role]
        energies[k] = energy
        meta[k, 0] = active.astype(jnp.int32)
        for column, orbital in ((1, x), (2, y)):
            slot = next(slot for slot, held in layout[role].values() if held == orbital)
            meta[k, column] = slot
            needed[role][slot] = needed[role][slot] | active
        meta[k, 3] = ("", "g0", "g1").index(left)
        meta[k, 4] = ("", "g0", "g1").index(right)
        meta[k, 5] = (place.lower if counted == "lower" else jnp.bool_(bool(counted))).astype(jnp.int32)
    run = functools.reduce(jnp.logical_or, [roles[role] for role in layout])
    held = {"g0": sums.at[0], "g1": sums.at[1], "density": square}
    uses = {name: run for name in held}

    def wanted(name, copies):
        @pl.when(uses[name])
        def _():
            copies(name)

    @pl.when(run)
    def _():
        state[0] = 0
        for s in range(slots.shape[0]):
            meta[s, 6] = 0
        for role in layout:
            for name, (s, _) in layout[role].items():

                @pl.when(needed[role][s])
                def _():
                    meta[s, 6] = 1
                    pltpu.make_async_copy(slabs[name], slots.at[s], slabs_sem.at[s]).start()

        pltpu.make_async_copy(levels_ref, levels, sums_sem.at[0]).start()
        for q, name in enumerate(given):
            wanted(name, lambda name: pltpu.make_async_copy(before[name], held[name], sums_sem.at[q + 1]).start())
        if "g0" in made and "g0" not in given:
            sums[0] = jnp.zeros(sums.shape[1:], sums.dtype)

        def arrived():
            @pl.when(state[0] == 0)
            def _():
                pltpu.make_async_copy(levels_ref, levels, sums_sem.at[0]).wait()
                for q, name in enumerate(given):
                    wanted(name, lambda name: pltpu.make_async_copy(before[name], held[name], sums_sem.at[q + 1]).wait())
                state[0] = 1

        @pl.loop(0, len(tasks))
        def _(k):
            @pl.when(meta[k, 0] == 1)
            def _():
                @pl.loop(1, 3)
                def _(column):
                    s = meta[k, column]

                    @pl.when(meta[s, 6] == 1)
                    def _():
                        pltpu.make_async_copy(slabs[names[0]], slots.at[s], slabs_sem.at[s]).wait()
                        high, low = halves(slots[s])
                        split[s, :, 0:width] = high
                        split[s, :, width:2 * width] = low
                        split[s, :, 2 * width:3 * width] = high
                        meta[s, 6] = 0

                x, y = split.at[meta[k, 1]], split.at[meta[k, 2]]
                t_ref[...] = mul(x[:, width:], y[:, :2 * width], ROWS) + mul(x[:, :width], y[:, :width], ROWS)
                arrived()
                t = t_ref[...] / (energies[k] - levels[...])
                t_ref[...] = t
                high, low = halves(t)

                def onto(target, z, dims):
                    wide = mul(high, z[:, :2 * width], dims)
                    sums[target] += wide[:, :width] + wide[:, width:] + mul(low, z[:, :width], dims)

                if any(task[3] for task in tasks):

                    @pl.when(meta[k, 3] > 0)
                    def _():
                        onto(meta[k, 3] - 1, y, PLAIN)

                if any(task[4] for task in tasks):

                    @pl.when(meta[k, 4] > 0)
                    def _():
                        onto(meta[k, 4] - 1, x, COLUMNS)

                if any(task[5] for task in tasks):

                    @pl.when(meta[k, 5] == 1)
                    def _():
                        square[...] += half_squares(t_ref[...])

        arrived()
        for q, name in enumerate(made):
            wanted(name, lambda name: pltpu.make_async_copy(held[name], after[name], sums_sem.at[q]).start())
        for q, name in enumerate(made):
            wanted(name, lambda name: pltpu.make_async_copy(held[name], after[name], sums_sem.at[q]).wait())


def count_kernel(density_ref, out_ref):
    total = density_ref[...]
    out_ref[...] = total + total.T


def home_sum_kernel(nocc, energy_ref, mask_ref, own_ref, late_ref, early_ref, out_ref, slots, own_sem, sum_sem, out_sem):
    place = Place(nocc, energy_ref, mask_ref)
    step = own_ref.shape[0] // PIECES

    def add(source):
        pieces = [pl.ds(p * step, step) for p in range(PIECES)]

        def own(p):
            return pltpu.make_async_copy(own_ref.at[pieces[p]], slots.at[0, pieces[p]], own_sem.at[p])

        def other(p):
            return pltpu.make_async_copy(source.at[pieces[p]], slots.at[1, pieces[p]], sum_sem.at[p])

        def out(p):
            return pltpu.make_async_copy(slots.at[0, pieces[p]], out_ref.at[pieces[p]], out_sem.at[p])

        for p in range(PIECES):
            own(p).start()
            other(p).start()
        for p in range(PIECES):
            own(p).wait()
            other(p).wait()
            slots[0, pieces[p]] += slots[1, pieces[p]]
            out(p).start()
        for p in range(PIECES):
            out(p).wait()

    @pl.when(place.from_late)
    def _():
        add(late_ref)

    @pl.when(place.from_early)
    def _():
        add(early_ref)


def body(slabs, occ_energy, vir_energy, pair_mask):
    nocc, ngrp = lax.axis_size("occ"), lax.axis_size("grp")
    routes = plan(nocc)
    own = slabs[0]
    rows, width = own.shape
    slab = jax.ShapeDtypeStruct((rows, width), jnp.float32)
    square = jax.ShapeDtypeStruct((rows, rows), jnp.float32)
    shapes = {"g0": slab, "g1": slab, "density": square}
    cost = pl.CostEstimate(flops=1000, bytes_accessed=1000, transcendentals=0)
    params = pltpu.CompilerParams(vmem_limit_bytes=VMEM_LIMIT)

    def pairs(tasks, there, given, made, fresh=()):
        inputs = [levels, *there.values(), *given.values()]
        first = 2 + len(inputs) - len(given)
        count = max(len(held) for held in slots_of(tasks).values())
        return pl.pallas_call(
            functools.partial(pairs_kernel, nocc, tasks, list(there), list(given), made),
            out_shape=[shapes[name] for name in made],
            in_specs=[SMEM, SMEM] + [ANY] * len(inputs),
            out_specs=[ANY] * len(made),
            scratch_shapes=[
                pltpu.VMEM((count, rows, width), jnp.float32),
                pltpu.VMEM((count, rows, 3 * width), jnp.bfloat16),
                pltpu.SemaphoreType.DMA((count,)),
                pltpu.VMEM((2, rows, width), jnp.float32),
                pltpu.VMEM((rows, rows), jnp.float32),
                pltpu.VMEM((rows, rows), jnp.float32),
                pltpu.VMEM((rows, rows), jnp.float32),
                pltpu.SemaphoreType.DMA((4,)),
                pltpu.SMEM((max(len(tasks), count), 8), jnp.int32),
                pltpu.SMEM((len(tasks),), jnp.float32),
                pltpu.SMEM((1,), jnp.int32),
            ],
            input_output_aliases={first + q: made.index(n) for q, n in enumerate(given) if n not in fresh},
            compiler_params=params,
            cost_estimate=cost,
            name="pairs",
        )(occ_energy, pair_mask, *inputs)

    early2 = move(own, routes["early2"])
    late0 = move(own, routes["late0"])
    home_grad, home_density, levels = pl.pallas_call(
        functools.partial(home_kernel, nocc),
        out_shape=[slab, square, square],
        in_specs=[SMEM, SMEM, VMEM, VMEM],
        out_specs=[VMEM] * 3,
        compiler_params=params,
        cost_estimate=cost,
        name="home_pair",
    )(occ_energy, pair_mask, vir_energy.reshape(1, rows), own)
    late0 = tied(late0, home_density)
    early3 = move(late0, routes["early2"])
    early0 = move(tied(own, late0), routes["early0"])
    late_p2 = move(tied(early2, home_density), routes["before"])
    g0, g1, density = pairs(
        [("early", "a1", "a2", "g1", "", "all"), ("late", "a0", "a1", "g0", "g1", "all")],
        {"own": own, "early2": early2, "late0": late0},
        {"g1": home_grad, "density": home_density},
        ["g0", "g1", "density"],
    )
    late2 = move(tied(own, g1), routes["late2"])
    early3 = tied(early3, g1)
    late_p3 = move(early3, routes["before"])
    g0, g1, density = pairs(
        [
            ("early", "a1", "a3", "g1", "", "all"),
            ("late", "a0", "p2", "g0", "", "all"),
        ],
        {"own": own, "early3": early3, "late0": late0, "late_p2": late_p2},
        {"g0": g0, "g1": g1, "density": density},
        ["g0", "g1", "density"],
    )
    early_p3 = move(tied(own, g1), routes["early_p3"])
    late2 = tied(late2, g1)
    early_p2 = move(late2, routes["to_early"])
    g0, g1, density = pairs(
        [
            ("early", "a0", "a2", "g0", "", "all"),
            ("early", "a0", "a1", "g0", "g1", "all"),
            ("early", "a0", "p2", "g0", "", "all"),
            ("late", "a0", "a2", "g0", "", ""),
            ("late", "a0", "p3", "g0", "", "lower"),
        ],
        {
            "own": own, "early0": early0, "early2": early2, "early_p2": early_p2, "late0": late0, "late2": late2,
            "late_p3": tied(late_p3, g1),
        },
        {"g0": g0, "g1": g1, "density": density},
        ["g0", "g1", "density"],
    )
    late_home = move(g0, routes["late_home"])
    (g1,) = pairs(
        [("late", "a1", "a2", "g1", "", ""), ("late", "a1", "p3", "g1", "", "")],
        {"own": own, "late2": late2, "late_p3": late_p3},
        {"g1": tied(g1, g0)},
        ["g1"],
    )
    early_p3 = tied(early_p3, g1)
    g0, density = pairs(
        [("early", "a0", "p3", "g0", "", "lower")],
        {"early0": early0, "early_p3": early_p3},
        {"g0": g0, "density": density},
        ["g0", "density"],
        fresh=("g0",),
    )
    early_home = move(g0, routes["early_home"])
    late3 = move(tied(early_p3, g0), routes["to_late"])
    density = pl.pallas_call(
        count_kernel, out_shape=square, compiler_params=params, cost_estimate=cost, name="count"
    )(density)

    def meanwhile(earlier):
        (grad,) = pairs(
            [("early", "a1", "p3", "g1", "", ""), ("late", "a1", "a3", "g1", "", "")],
            {"own": own, "early_p3": early_p3, "late3": late3},
            {"g1": tied(g1, earlier)},
            ["g1"],
        )
        return pl.pallas_call(
            functools.partial(home_sum_kernel, nocc),
            out_shape=slab,
            in_specs=[SMEM, SMEM, ANY, ANY, ANY],
            out_specs=ANY,
            scratch_shapes=[
                pltpu.VMEM((2, rows, width), jnp.float32),
                pltpu.SemaphoreType.DMA((PIECES,)),
                pltpu.SemaphoreType.DMA((PIECES,)),
                pltpu.SemaphoreType.DMA((PIECES,)),
            ],
            input_output_aliases={2: 0},
            compiler_params=params,
            cost_estimate=cost,
            name="home_sum",
        )(occ_energy, pair_mask, grad, late_home, early_home)

    blocks, gradient = reduced(density, nocc, ngrp, meanwhile, late_home)
    return gradient[None], blocks / (nocc * ngrp)


def combined(parts):
    while len(parts) > 1:
        parts = [x + y for x, y in zip(parts[::2], parts[1::2])]
    return parts[0]


def reduced(density, nocc, ngrp, meanwhile, arriving):
    place = lax.axis_index("occ")
    width = density.shape[1]
    rows = density.shape[0] // nocc
    blocks = density
    bit, radix = 1, 2
    while bit < nocc:
        radix = min(radix, nocc // bit)
        blocks = blocks.reshape(-1, radix, rows, width)
        digit = (place // bit) % radix
        received = []
        for j in range(radix):
            part = lax.dynamic_index_in_dim(blocks, digit ^ j, 1, keepdims=False)
            if j:
                part = lax.ppermute(part, "occ", [(o, o ^ (j * bit)) for o in range(nocc)])
            received.append(part)
        if bit == 1:
            received = lax.optimization_barrier((*received, arriving))[:-1]
        blocks = combined(received)
        bit, radix = bit * radix, 4
    blocks = blocks.reshape(rows, width)
    others = [lax.ppermute(blocks, "grp", [(g, g ^ j) for g in range(ngrp)]) for j in range(1, ngrp)]
    made = meanwhile(blocks)
    others = lax.optimization_barrier((*others, made))[:-1]
    return combined([blocks, *others]), made


def solution(mesh):
    nocc = mesh.shape["occ"]
    if mesh.shape["grp"] != 4 or nocc < 4 or nocc & (nocc - 1):
        raise NotImplementedError("another mesh")
    placed = (P(AXES, None, None), P(), P(), P())
    return jax.shard_map(
        body,
        mesh=mesh,
        in_specs=placed,
        out_specs=(P(AXES, None, None), P("occ", None)),
        check_vma=False,
    )
```

```python
import functools

import jax
import jax.numpy as jnp
from jax import lax
from jax.experimental import pallas as pl
from jax.experimental.pallas import tpu as pltpu
from jax.sharding import PartitionSpec as P

AXES = ("occ", "grp")
PIECES = 4
VMEM_LIMIT = 56 * 1024 * 1024

SMEM = pl.BlockSpec(memory_space=pltpu.SMEM)
VMEM = pl.BlockSpec(memory_space=pltpu.VMEM)
ANY = pl.BlockSpec(memory_space=pl.ANY)


def plan(nocc):
    names = ("early2", "late0", "early0", "late2", "early_p3", "to_early", "to_late", "early_home", "late_home", "before")
    routes = {name: [] for name in names}

    def both(name, source, target):
        routes[name].append(tuple(4 * block + place for block, place in (source, target)))
        routes[name].append(tuple(4 * (nocc - 1 - block) + 3 - place for block, place in (source, target)))

    for even in range(0, nocc, 2):
        odd = even + 1
        both("early2", (odd, 2), (odd, 1))
        both("late0", (even, 0), (even, 1))
        both("early0", (odd, 0), (odd, 1))
        both("late2", (even, 2), (even, 1))
        both("early_p3", (even, 3), (odd, 1))
        both("to_early", (even, 1), (odd, 1))
        both("to_late", (odd, 1), (even, 1))
        both("early_home", (odd, 1), (odd, 0))
        both("late_home", (even, 1), (even, 0))
        if even:
            both("before", (even - 1, 1), (even, 1))
    return routes


def move(block, route):
    return lax.ppermute(block, AXES, route)


def tied(x, *earlier):
    return lax.optimization_barrier((x, *earlier))[0]


class Place:
    def __init__(self, nocc, energy_ref, mask_ref):
        occ, grp = lax.axis_index("occ"), lax.axis_index("grp")
        self.energy_ref, self.mask_ref = energy_ref, mask_ref
        self.last = nocc * 4 - 1
        self.own = occ * 4 + grp
        self.lower = grp <= 1
        hub = (grp == 1) | (grp == 2)
        inner = (lax.rem(occ, 2) == 1) == self.lower
        self.early, self.late = hub & inner, hub & ~inner
        self.from_late, self.from_early = ~hub & ~inner, ~hub & inner
        step = jnp.where(self.lower, 1, -1)
        a0 = occ * 4 + jnp.where(self.lower, 0, 3)
        self.index = {"a0": a0, "a1": a0 + step, "a2": a0 + 2 * step, "a3": a0 + 3 * step, "p3": a0 - step, "p2": a0 - 2 * step}

    def pair(self, x, y):
        offset = {"a0a1": 1, "a0a2": 2, "a1a2": 1, "a1a3": 2, "a0p2": 2, "a0p3": 1, "a1p3": 2}[x + y]
        i, j = self.index[x], self.index[y]
        there = (j >= 0) & (j <= self.last)
        i, j = jnp.clip(i, 0, self.last), jnp.clip(j, 0, self.last)
        active = there & (self.mask_ref[jnp.minimum(i, j), offset - 1] == 1)
        return active, self.energy_ref[i] + self.energy_ref[j]


ROWS = ((1,), (1,))
PLAIN = ((1,), (0,))
COLUMNS = ((0,), (0,))


def mul(left, right, dims):
    return lax.dot_general(left, right, (dims, ((), ())), preferred_element_type=jnp.float32)


def halves(x):
    high = x.astype(jnp.bfloat16)
    return high, (x - high.astype(jnp.float32)).astype(jnp.bfloat16)


def parts(x, other, axis):
    high, low = halves(x)
    return jnp.concatenate([high, low, high] if other else [high, high, low], axis)


def half_squares(t):
    high, low = halves(t)
    left, right = [high, high], [high * 0.5, low]
    return mul(jnp.concatenate(left, 1), jnp.concatenate(right, 1), ROWS) + mul(
        jnp.concatenate(left, 0), jnp.concatenate(right, 0), COLUMNS
    )


def home_kernel(nocc, energy_ref, mask_ref, vir_ref, slab_ref, grad_ref, density_ref, levels_ref):
    rows = slab_ref.shape[0]
    spread = jnp.broadcast_to(vir_ref[...], (rows, rows))
    levels_ref[...] = spread + spread.T
    energy = energy_ref[Place(nocc, energy_ref, mask_ref).own]
    slab = slab_ref[...]
    t = mul(parts(slab, False, 1), parts(slab, True, 1), ROWS) / (2.0 * energy - levels_ref[...])
    t3 = parts(t, False, 1)
    grad_ref[...] = 2.0 * mul(t3, parts(slab, True, 0), PLAIN)
    density_ref[...] = mul(t3, parts(t, True, 1), ROWS)


def slots_of(tasks):
    found = {}
    for role, x, y, *_ in tasks:
        for orbital in (x, y):
            name = "own" if orbital == "a1" else role + orbital[1:] if orbital[0] == "a" else role + "_" + orbital
            if name not in found.setdefault(role, {}):
                found[role][name] = (len(found[role]), orbital)
    return found


def pairs_kernel(nocc, tasks, names, given, made, fresh, energy_ref, mask_ref, levels_ref, *refs):
    slabs, refs = dict(zip(names, refs[:len(names)])), refs[len(names):]
    before, refs = dict(zip(given, refs[:len(given)])), refs[len(given):]
    after, refs = dict(zip(made, refs[:len(made)])), refs[len(made):]
    slots, split, slabs_sem, sums, square, levels, t_ref, sums_sem, meta, energies, state = refs
    width = slots.shape[2]
    place = Place(nocc, energy_ref, mask_ref)
    roles = {"early": place.early, "late": place.late}
    layout = slots_of(tasks)
    added = {name: jnp.bool_(False) for name in ("g0", "g1", "density")}
    needed = {role: [jnp.bool_(False)] * len(layout[role]) for role in layout}
    for k, (role, x, y, left, right, counted) in enumerate(tasks):
        active, energy = place.pair(x, y)
        active = active & roles[role]
        energies[k] = energy
        meta[k, 0] = active.astype(jnp.int32)
        for column, orbital in ((1, x), (2, y)):
            slot = next(slot for slot, held in layout[role].values() if held == orbital)
            meta[k, column] = slot
            needed[role][slot] = needed[role][slot] | active
        meta[k, 3] = ("", "g0", "g1").index(left)
        meta[k, 4] = ("", "g0", "g1").index(right)
        counts = place.lower if counted == "lower" else jnp.bool_(bool(counted))
        for name, used in ((left, active), (right, active), ("density", active & counts)):
            if name:
                added[name] = added[name] | used
        meta[k, 5] = counts.astype(jnp.int32)
    run = functools.reduce(jnp.logical_or, [roles[role] for role in layout])
    held = {"g0": sums.at[0], "g1": sums.at[1], "density": square}
    uses = {name: run if name in fresh or name not in given else added[name] for name in made}

    def wanted(name, copies):
        @pl.when(uses[name])
        def _():
            copies(name)

    @pl.when(run)
    def _():
        state[0] = 0
        for s in range(slots.shape[0]):
            meta[s, 6] = 0
        for role in layout:
            for name, (s, _) in layout[role].items():

                @pl.when(needed[role][s])
                def _():
                    meta[s, 6] = 1
                    pltpu.make_async_copy(slabs[name], slots.at[s], slabs_sem.at[s]).start()

        pltpu.make_async_copy(levels_ref, levels, sums_sem.at[0]).start()
        for q, name in enumerate(given):
            wanted(name, lambda name: pltpu.make_async_copy(before[name], held[name], sums_sem.at[q + 1]).start())
        if "g0" in made and "g0" not in given:
            sums[0] = jnp.zeros(sums.shape[1:], sums.dtype)

        def arrived():
            @pl.when(state[0] == 0)
            def _():
                pltpu.make_async_copy(levels_ref, levels, sums_sem.at[0]).wait()
                for q, name in enumerate(given):
                    wanted(name, lambda name: pltpu.make_async_copy(before[name], held[name], sums_sem.at[q + 1]).wait())
                state[0] = 1

        @pl.loop(0, len(tasks))
        def _(k):
            @pl.when(meta[k, 0] == 1)
            def _():
                @pl.loop(1, 3)
                def _(column):
                    s = meta[k, column]

                    @pl.when(meta[s, 6] == 1)
                    def _():
                        pltpu.make_async_copy(slabs[names[0]], slots.at[s], slabs_sem.at[s]).wait()
                        high, low = halves(slots[s])
                        split[s, :, 0:width] = high
                        split[s, :, width:2 * width] = low
                        split[s, :, 2 * width:3 * width] = high
                        meta[s, 6] = 0

                x, y = split.at[meta[k, 1]], split.at[meta[k, 2]]
                t_ref[...] = mul(x[:, width:], y[:, :2 * width], ROWS) + mul(x[:, :width], y[:, :width], ROWS)
                arrived()
                t = t_ref[...] / (energies[k] - levels[...])
                t_ref[...] = t
                high, low = halves(t)

                def onto(target, z, dims):
                    wide = mul(high, z[:, :2 * width], dims)
                    sums[target] += wide[:, :width] + wide[:, width:] + mul(low, z[:, :width], dims)

                if any(task[3] for task in tasks):

                    @pl.when(meta[k, 3] > 0)
                    def _():
                        onto(meta[k, 3] - 1, y, PLAIN)

                if any(task[4] for task in tasks):

                    @pl.when(meta[k, 4] > 0)
                    def _():
                        onto(meta[k, 4] - 1, x, COLUMNS)

                if any(task[5] for task in tasks):

                    @pl.when(meta[k, 5] == 1)
                    def _():
                        square[...] += half_squares(t_ref[...])

        arrived()
        for q, name in enumerate(made):
            wanted(name, lambda name: pltpu.make_async_copy(held[name], after[name], sums_sem.at[q]).start())
        for q, name in enumerate(made):
            wanted(name, lambda name: pltpu.make_async_copy(held[name], after[name], sums_sem.at[q]).wait())


def count_kernel(density_ref, out_ref):
    total = density_ref[...]
    out_ref[...] = total + total.T


def home_sum_kernel(nocc, energy_ref, mask_ref, own_ref, late_ref, early_ref, out_ref, slots, own_sem, sum_sem, out_sem):
    place = Place(nocc, energy_ref, mask_ref)
    step = own_ref.shape[0] // PIECES

    def add(source):
        pieces = [pl.ds(p * step, step) for p in range(PIECES)]

        def own(p):
            return pltpu.make_async_copy(own_ref.at[pieces[p]], slots.at[0, pieces[p]], own_sem.at[p])

        def other(p):
            return pltpu.make_async_copy(source.at[pieces[p]], slots.at[1, pieces[p]], sum_sem.at[p])

        def out(p):
            return pltpu.make_async_copy(slots.at[0, pieces[p]], out_ref.at[pieces[p]], out_sem.at[p])

        for p in range(PIECES):
            own(p).start()
            other(p).start()
        for p in range(PIECES):
            own(p).wait()
            other(p).wait()
            slots[0, pieces[p]] += slots[1, pieces[p]]
            out(p).start()
        for p in range(PIECES):
            out(p).wait()

    @pl.when(place.from_late)
    def _():
        add(late_ref)

    @pl.when(place.from_early)
    def _():
        add(early_ref)


def body(slabs, occ_energy, vir_energy, pair_mask):
    nocc, ngrp = lax.axis_size("occ"), lax.axis_size("grp")
    routes = plan(nocc)
    own = slabs[0]
    rows, width = own.shape
    slab = jax.ShapeDtypeStruct((rows, width), jnp.float32)
    square = jax.ShapeDtypeStruct((rows, rows), jnp.float32)
    shapes = {"g0": slab, "g1": slab, "density": square}
    cost = pl.CostEstimate(flops=1000, bytes_accessed=1000, transcendentals=0)
    params = pltpu.CompilerParams(vmem_limit_bytes=VMEM_LIMIT)

    def pairs(tasks, there, given, made, fresh=()):
        inputs = [levels, *there.values(), *given.values()]
        first = 2 + len(inputs) - len(given)
        count = max(len(held) for held in slots_of(tasks).values())
        return pl.pallas_call(
            functools.partial(pairs_kernel, nocc, tasks, list(there), list(given), made, fresh),
            out_shape=[shapes[name] for name in made],
            in_specs=[SMEM, SMEM] + [ANY] * len(inputs),
            out_specs=[ANY] * len(made),
            scratch_shapes=[
                pltpu.VMEM((count, rows, width), jnp.float32),
                pltpu.VMEM((count, rows, 3 * width), jnp.bfloat16),
                pltpu.SemaphoreType.DMA((count,)),
                pltpu.VMEM((2, rows, width), jnp.float32),
                pltpu.VMEM((rows, rows), jnp.float32),
                pltpu.VMEM((rows, rows), jnp.float32),
                pltpu.VMEM((rows, rows), jnp.float32),
                pltpu.SemaphoreType.DMA((4,)),
                pltpu.SMEM((max(len(tasks), count), 8), jnp.int32),
                pltpu.SMEM((len(tasks),), jnp.float32),
                pltpu.SMEM((1,), jnp.int32),
            ],
            input_output_aliases={first + q: made.index(n) for q, n in enumerate(given) if n not in fresh},
            compiler_params=params,
            cost_estimate=cost,
            name="pairs",
        )(occ_energy, pair_mask, *inputs)

    early2 = move(own, routes["early2"])
    late0 = move(own, routes["late0"])
    home_grad, home_density, levels = pl.pallas_call(
        functools.partial(home_kernel, nocc),
        out_shape=[slab, square, square],
        in_specs=[SMEM, SMEM, VMEM, VMEM],
        out_specs=[VMEM] * 3,
        compiler_params=params,
        cost_estimate=cost,
        name="home_pair",
    )(occ_energy, pair_mask, vir_energy.reshape(1, rows), own)
    late0 = tied(late0, home_density)
    early3 = move(late0, routes["early2"])
    early0 = move(tied(own, late0), routes["early0"])
    late_p2 = move(tied(early2, home_density), routes["before"])
    g0, g1, density = pairs(
        [("early", "a1", "a2", "g1", "", "all"), ("late", "a0", "a1", "g0", "g1", "all")],
        {"own": own, "early2": early2, "late0": late0},
        {"g1": home_grad, "density": home_density},
        ["g0", "g1", "density"],
    )
    early3 = tied(early3, g1)
    late2 = move(tied(own, early3), routes["late2"])
    late_p3 = move(early3, routes["before"])
    g0, g1, density = pairs(
        [
            ("early", "a1", "a3", "g1", "", "all"),
            ("early", "a0", "a1", "g0", "g1", "all"),
            ("late", "a0", "p2", "g0", "", "all"),
        ],
        {"own": own, "early0": early0, "early3": early3, "late0": late0, "late_p2": late_p2},
        {"g0": g0, "g1": g1, "density": density},
        ["g0", "g1", "density"],
    )
    early_p3 = move(tied(own, g1), routes["early_p3"])
    late2 = tied(late2, g1)
    early_p2 = move(late2, routes["to_early"])
    g0, density = pairs(
        [
            ("early", "a0", "a2", "g0", "", "all"),
            ("early", "a0", "p2", "g0", "", "all"),
            ("late", "a0", "a2", "g0", "", ""),
            ("late", "a0", "p3", "g0", "", "lower"),
        ],
        {
            "early0": early0, "early2": early2, "early_p2": early_p2, "late0": late0, "late2": late2,
            "late_p3": tied(late_p3, g1),
        },
        {"g0": g0, "density": density},
        ["g0", "density"],
    )
    late_home = move(g0, routes["late_home"])
    (g1,) = pairs(
        [("late", "a1", "a2", "g1", "", ""), ("late", "a1", "p3", "g1", "", "")],
        {"own": own, "late2": late2, "late_p3": late_p3},
        {"g1": tied(g1, g0)},
        ["g1"],
    )
    early_p3 = tied(early_p3, g1)
    g0, density = pairs(
        [("early", "a0", "p3", "g0", "", "lower")],
        {"early0": early0, "early_p3": early_p3},
        {"g0": g0, "density": density},
        ["g0", "density"],
        fresh=("g0",),
    )
    early_home = move(g0, routes["early_home"])
    late3 = move(tied(early_p3, g0), routes["to_late"])
    density = pl.pallas_call(
        count_kernel, out_shape=square, compiler_params=params, cost_estimate=cost, name="count"
    )(density)

    def meanwhile(earlier):
        (grad,) = pairs(
            [("early", "a1", "p3", "g1", "", "")], {"own": own, "early_p3": early_p3}, {"g1": tied(g1, earlier)}, ["g1"]
        )
        grad = pl.pallas_call(
            functools.partial(home_sum_kernel, nocc),
            out_shape=slab,
            in_specs=[SMEM, SMEM, ANY, ANY, ANY],
            out_specs=ANY,
            scratch_shapes=[
                pltpu.VMEM((2, rows, width), jnp.float32),
                pltpu.SemaphoreType.DMA((PIECES,)),
                pltpu.SemaphoreType.DMA((PIECES,)),
                pltpu.SemaphoreType.DMA((PIECES,)),
            ],
            input_output_aliases={2: 0},
            compiler_params=params,
            cost_estimate=cost,
            name="home_sum",
        )(occ_energy, pair_mask, grad, late_home, early_home)
        return pairs([("late", "a1", "a3", "g1", "", "")], {"own": own, "late3": late3}, {"g1": grad}, ["g1"])[0]

    blocks, gradient = reduced(density, nocc, ngrp, meanwhile, late_home)
    return gradient[None], blocks / (nocc * ngrp)


def combined(parts):
    while len(parts) > 1:
        parts = [x + y for x, y in zip(parts[::2], parts[1::2])]
    return parts[0]


def reduced(density, nocc, ngrp, meanwhile, arriving):
    place = lax.axis_index("occ")
    width = density.shape[1]
    rows = density.shape[0] // nocc
    blocks = density
    bit, radix = 1, 2
    while bit < nocc:
        radix = min(radix, nocc // bit)
        blocks = blocks.reshape(-1, radix, rows, width)
        digit = (place // bit) % radix
        received = []
        for j in range(radix):
            part = lax.dynamic_index_in_dim(blocks, digit ^ j, 1, keepdims=False)
            if j:
                part = lax.ppermute(part, "occ", [(o, o ^ (j * bit)) for o in range(nocc)])
            received.append(part)
        blocks = combined(received)
        bit, radix = bit * radix, 4
    blocks = tied(blocks.reshape(rows, width), arriving)
    others = [lax.ppermute(blocks, "grp", [(g, g ^ j) for g in range(ngrp)]) for j in range(1, ngrp)]
    made = meanwhile(blocks)
    others = lax.optimization_barrier((*others, made))[:-1]
    return combined([blocks, *others]), made


def solution(mesh):
    nocc = mesh.shape["occ"]
    if mesh.shape["grp"] != 4 or nocc < 4 or nocc & (nocc - 1):
        raise NotImplementedError("another mesh")
    placed = (P(AXES, None, None), P(), P(), P())
    return jax.shard_map(
        body,
        mesh=mesh,
        in_specs=placed,
        out_specs=(P(AXES, None, None), P("occ", None)),
        check_vma=False,
    )
```

```python
import functools

import jax
import jax.numpy as jnp
from jax import lax
from jax.experimental import pallas as pl
from jax.experimental.pallas import tpu as pltpu
from jax.sharding import PartitionSpec as P

AXES = ("occ", "grp")
PIECES = 4
VMEM_LIMIT = 63 * 1024 * 1024

SMEM = pl.BlockSpec(memory_space=pltpu.SMEM)
VMEM = pl.BlockSpec(memory_space=pltpu.VMEM)
ANY = pl.BlockSpec(memory_space=pl.ANY)


def plan(nocc):
    names = ("early2", "late0", "early0", "late2", "early_p3", "to_early", "to_late", "early_home", "late_home", "before")
    routes = {name: [] for name in names}

    def both(name, source, target):
        routes[name].append(tuple(4 * block + place for block, place in (source, target)))
        routes[name].append(tuple(4 * (nocc - 1 - block) + 3 - place for block, place in (source, target)))

    for even in range(0, nocc, 2):
        odd = even + 1
        both("early2", (odd, 2), (odd, 1))
        both("late0", (even, 0), (even, 1))
        both("early0", (odd, 0), (odd, 1))
        both("late2", (even, 2), (even, 1))
        both("early_p3", (even, 3), (odd, 1))
        both("to_early", (even, 1), (odd, 1))
        both("to_late", (odd, 1), (even, 1))
        both("early_home", (odd, 1), (odd, 0))
        both("late_home", (even, 1), (even, 0))
        if even:
            both("before", (even - 1, 1), (even, 1))
    return routes


def move(block, route):
    return lax.ppermute(block, AXES, route)


def tied(x, *earlier):
    return lax.optimization_barrier((x, *earlier))[0]


class Place:
    def __init__(self, nocc, energy_ref, mask_ref):
        occ, grp = lax.axis_index("occ"), lax.axis_index("grp")
        self.energy_ref, self.mask_ref = energy_ref, mask_ref
        self.last = nocc * 4 - 1
        self.own = occ * 4 + grp
        self.lower = grp <= 1
        hub = (grp == 1) | (grp == 2)
        inner = (lax.rem(occ, 2) == 1) == self.lower
        self.early, self.late = hub & inner, hub & ~inner
        self.from_late, self.from_early = ~hub & ~inner, ~hub & inner
        step = jnp.where(self.lower, 1, -1)
        a0 = occ * 4 + jnp.where(self.lower, 0, 3)
        self.index = {"a0": a0, "a1": a0 + step, "a2": a0 + 2 * step, "a3": a0 + 3 * step, "p3": a0 - step, "p2": a0 - 2 * step}

    def pair(self, x, y):
        offset = {"a0a1": 1, "a0a2": 2, "a1a2": 1, "a1a3": 2, "a0p2": 2, "a0p3": 1, "a1p3": 2}[x + y]
        i, j = self.index[x], self.index[y]
        there = (j >= 0) & (j <= self.last)
        i, j = jnp.clip(i, 0, self.last), jnp.clip(j, 0, self.last)
        active = there & (self.mask_ref[jnp.minimum(i, j), offset - 1] == 1)
        return active, self.energy_ref[i] + self.energy_ref[j]


ROWS = ((1,), (1,))
PLAIN = ((1,), (0,))
COLUMNS = ((0,), (0,))


def mul(left, right, dims):
    return lax.dot_general(left, right, (dims, ((), ())), preferred_element_type=jnp.float32)


def halves(x):
    high = x.astype(jnp.bfloat16)
    return high, (x - high.astype(jnp.float32)).astype(jnp.bfloat16)


def parts(x, other, axis):
    high, low = halves(x)
    return jnp.concatenate([high, low, high] if other else [high, high, low], axis)


def half_squares(t):
    high, low = halves(t)
    left, right = [high, high], [high * 0.5, low]
    return mul(jnp.concatenate(left, 1), jnp.concatenate(right, 1), ROWS) + mul(
        jnp.concatenate(left, 0), jnp.concatenate(right, 0), COLUMNS
    )


def home_kernel(nocc, energy_ref, mask_ref, vir_ref, slab_ref, grad_ref, density_ref, levels_ref):
    rows = slab_ref.shape[0]
    spread = jnp.broadcast_to(vir_ref[...], (rows, rows))
    levels_ref[...] = spread + spread.T
    energy = energy_ref[Place(nocc, energy_ref, mask_ref).own]
    slab = slab_ref[...]
    t = mul(parts(slab, False, 1), parts(slab, True, 1), ROWS) / (2.0 * energy - levels_ref[...])
    t3 = parts(t, False, 1)
    grad_ref[...] = 2.0 * mul(t3, parts(slab, True, 0), PLAIN)
    density_ref[...] = mul(t3, parts(t, True, 1), ROWS)


def slots_of(tasks):
    found = {}
    for role, x, y, *_ in tasks:
        for orbital in (x, y):
            name = "own" if orbital == "a1" else role + orbital[1:] if orbital[0] == "a" else role + "_" + orbital
            if name not in found.setdefault(role, {}):
                found[role][name] = (len(found[role]), orbital)
    return found


def pairs_kernel(nocc, tasks, names, given, made, fresh, energy_ref, mask_ref, levels_ref, *refs):
    slabs, refs = dict(zip(names, refs[:len(names)])), refs[len(names):]
    before, refs = dict(zip(given, refs[:len(given)])), refs[len(given):]
    after, refs = dict(zip(made, refs[:len(made)])), refs[len(made):]
    slots, split, slabs_sem, sums, square, levels, t_ref, sums_sem, meta, energies, state = refs
    width = slots.shape[2]
    place = Place(nocc, energy_ref, mask_ref)
    roles = {"early": place.early, "late": place.late}
    layout = slots_of(tasks)
    added = {name: jnp.bool_(False) for name in ("g0", "g1", "density")}
    needed = {role: [jnp.bool_(False)] * len(layout[role]) for role in layout}
    for k, (role, x, y, left, right, counted) in enumerate(tasks):
        active, energy = place.pair(x, y)
        active = active & roles[role]
        energies[k] = energy
        meta[k, 0] = active.astype(jnp.int32)
        for column, orbital in ((1, x), (2, y)):
            slot = next(slot for slot, held in layout[role].values() if held == orbital)
            meta[k, column] = slot
            needed[role][slot] = needed[role][slot] | active
        meta[k, 3] = ("", "g0", "g1").index(left)
        meta[k, 4] = ("", "g0", "g1").index(right)
        counts = place.lower if counted == "lower" else jnp.bool_(bool(counted))
        for name, used in ((left, active), (right, active), ("density", active & counts)):
            if name:
                added[name] = added[name] | used
        meta[k, 5] = counts.astype(jnp.int32)
    run = functools.reduce(jnp.logical_or, [roles[role] for role in layout])
    held = {"g0": sums.at[0], "g1": sums.at[1], "density": square}
    uses = {name: run if name in fresh or name not in given else added[name] for name in made}

    def wanted(name, copies):
        @pl.when(uses[name])
        def _():
            copies(name)

    @pl.when(run)
    def _():
        state[0] = 0
        for s in range(slots.shape[0]):
            meta[s, 6] = 0
        for role in layout:
            for name, (s, _) in layout[role].items():

                @pl.when(needed[role][s])
                def _():
                    meta[s, 6] = 1
                    pltpu.make_async_copy(slabs[name], slots.at[s], slabs_sem.at[s]).start()

        pltpu.make_async_copy(levels_ref, levels, sums_sem.at[0]).start()
        for q, name in enumerate(given):
            wanted(name, lambda name: pltpu.make_async_copy(before[name], held[name], sums_sem.at[q + 1]).start())
        if "g0" in made and "g0" not in given:
            sums[0] = jnp.zeros(sums.shape[1:], sums.dtype)

        def arrived():
            @pl.when(state[0] == 0)
            def _():
                pltpu.make_async_copy(levels_ref, levels, sums_sem.at[0]).wait()
                for q, name in enumerate(given):
                    wanted(name, lambda name: pltpu.make_async_copy(before[name], held[name], sums_sem.at[q + 1]).wait())
                state[0] = 1

        @pl.loop(0, len(tasks))
        def _(k):
            @pl.when(meta[k, 0] == 1)
            def _():
                @pl.loop(1, 3)
                def _(column):
                    s = meta[k, column]

                    @pl.when(meta[s, 6] == 1)
                    def _():
                        pltpu.make_async_copy(slabs[names[0]], slots.at[s], slabs_sem.at[s]).wait()
                        high, low = halves(slots[s])
                        split[s, :, 0:width] = high
                        split[s, :, width:2 * width] = low
                        split[s, :, 2 * width:3 * width] = high
                        meta[s, 6] = 0

                x, y = split.at[meta[k, 1]], split.at[meta[k, 2]]
                t_ref[...] = mul(x[:, width:], y[:, :2 * width], ROWS) + mul(x[:, :width], y[:, :width], ROWS)
                arrived()
                t = t_ref[...] / (energies[k] - levels[...])
                t_ref[...] = t
                high, low = halves(t)

                def onto(target, z, dims):
                    wide = mul(high, z[:, :2 * width], dims)
                    sums[target] += wide[:, :width] + wide[:, width:] + mul(low, z[:, :width], dims)

                if any(task[3] for task in tasks):

                    @pl.when(meta[k, 3] > 0)
                    def _():
                        onto(meta[k, 3] - 1, y, PLAIN)

                if any(task[4] for task in tasks):

                    @pl.when(meta[k, 4] > 0)
                    def _():
                        onto(meta[k, 4] - 1, x, COLUMNS)

                if any(task[5] for task in tasks):

                    @pl.when(meta[k, 5] == 1)
                    def _():
                        square[...] += half_squares(t_ref[...])

        arrived()
        for q, name in enumerate(made):
            wanted(name, lambda name: pltpu.make_async_copy(held[name], after[name], sums_sem.at[q]).start())
        for q, name in enumerate(made):
            wanted(name, lambda name: pltpu.make_async_copy(held[name], after[name], sums_sem.at[q]).wait())


def count_kernel(density_ref, out_ref):
    total = density_ref[...]
    out_ref[...] = total + total.T


def home_sum_kernel(nocc, energy_ref, mask_ref, own_ref, late_ref, early_ref, out_ref, slots, own_sem, sum_sem, out_sem):
    place = Place(nocc, energy_ref, mask_ref)
    step = own_ref.shape[0] // PIECES

    def add(source):
        pieces = [pl.ds(p * step, step) for p in range(PIECES)]

        def own(p):
            return pltpu.make_async_copy(own_ref.at[pieces[p]], slots.at[0, pieces[p]], own_sem.at[p])

        def other(p):
            return pltpu.make_async_copy(source.at[pieces[p]], slots.at[1, pieces[p]], sum_sem.at[p])

        def out(p):
            return pltpu.make_async_copy(slots.at[0, pieces[p]], out_ref.at[pieces[p]], out_sem.at[p])

        for p in range(PIECES):
            own(p).start()
            other(p).start()
        for p in range(PIECES):
            own(p).wait()
            other(p).wait()
            slots[0, pieces[p]] += slots[1, pieces[p]]
            out(p).start()
        for p in range(PIECES):
            out(p).wait()

    @pl.when(place.from_late)
    def _():
        add(late_ref)

    @pl.when(place.from_early)
    def _():
        add(early_ref)


def body(slabs, occ_energy, vir_energy, pair_mask):
    nocc, ngrp = lax.axis_size("occ"), lax.axis_size("grp")
    routes = plan(nocc)
    own = slabs[0]
    rows, width = own.shape
    slab = jax.ShapeDtypeStruct((rows, width), jnp.float32)
    square = jax.ShapeDtypeStruct((rows, rows), jnp.float32)
    shapes = {"g0": slab, "g1": slab, "density": square}
    cost = pl.CostEstimate(flops=1000, bytes_accessed=1000, transcendentals=0)
    params = pltpu.CompilerParams(vmem_limit_bytes=VMEM_LIMIT)

    def pairs(tasks, there, given, made, fresh=()):
        inputs = [levels, *there.values(), *given.values()]
        first = 2 + len(inputs) - len(given)
        count = max(len(held) for held in slots_of(tasks).values())
        return pl.pallas_call(
            functools.partial(pairs_kernel, nocc, tasks, list(there), list(given), made, fresh),
            out_shape=[shapes[name] for name in made],
            in_specs=[SMEM, SMEM] + [ANY] * len(inputs),
            out_specs=[ANY] * len(made),
            scratch_shapes=[
                pltpu.VMEM((count, rows, width), jnp.float32),
                pltpu.VMEM((count, rows, 3 * width), jnp.bfloat16),
                pltpu.SemaphoreType.DMA((count,)),
                pltpu.VMEM((2, rows, width), jnp.float32),
                pltpu.VMEM((rows, rows), jnp.float32),
                pltpu.VMEM((rows, rows), jnp.float32),
                pltpu.VMEM((rows, rows), jnp.float32),
                pltpu.SemaphoreType.DMA((4,)),
                pltpu.SMEM((max(len(tasks), count), 8), jnp.int32),
                pltpu.SMEM((len(tasks),), jnp.float32),
                pltpu.SMEM((1,), jnp.int32),
            ],
            input_output_aliases={first + q: made.index(n) for q, n in enumerate(given) if n not in fresh},
            compiler_params=params,
            cost_estimate=cost,
            name="pairs",
        )(occ_energy, pair_mask, *inputs)

    early2 = move(own, routes["early2"])
    late0 = move(own, routes["late0"])
    home_grad, home_density, levels = pl.pallas_call(
        functools.partial(home_kernel, nocc),
        out_shape=[slab, square, square],
        in_specs=[SMEM, SMEM, VMEM, VMEM],
        out_specs=[VMEM] * 3,
        compiler_params=params,
        cost_estimate=cost,
        name="home_pair",
    )(occ_energy, pair_mask, vir_energy.reshape(1, rows), own)
    late0 = tied(late0, home_density)
    early3 = move(late0, routes["early2"])
    early0 = move(tied(own, late0), routes["early0"])
    late_p2 = move(tied(early2, home_density), routes["before"])
    g0, g1, density = pairs(
        [("early", "a1", "a2", "g1", "", "all"), ("late", "a0", "a1", "g0", "g1", "all")],
        {"own": own, "early2": early2, "late0": late0},
        {"g1": home_grad, "density": home_density},
        ["g0", "g1", "density"],
    )
    early3 = tied(early3, g1)
    late2 = move(tied(own, early3), routes["late2"])
    late_p3 = move(early3, routes["before"])
    g0, g1, density = pairs(
        [
            ("early", "a1", "a3", "g1", "", "all"),
            ("early", "a0", "a1", "g0", "g1", "all"),
            ("late", "a0", "p2", "g0", "", "all"),
        ],
        {"own": own, "early0": early0, "early3": early3, "late0": late0, "late_p2": late_p2},
        {"g0": g0, "g1": g1, "density": density},
        ["g0", "g1", "density"],
    )
    early_p3 = move(tied(own, g1), routes["early_p3"])
    late2 = tied(late2, g1)
    early_p2 = move(late2, routes["to_early"])
    g0, density = pairs(
        [
            ("early", "a0", "a2", "g0", "", "all"),
            ("early", "a0", "p2", "g0", "", "all"),
            ("late", "a0", "a2", "g0", "", ""),
            ("late", "a0", "p3", "g0", "", "lower"),
        ],
        {
            "early0": early0, "early2": early2, "early_p2": early_p2, "late0": late0, "late2": late2,
            "late_p3": tied(late_p3, g1),
        },
        {"g0": g0, "density": density},
        ["g0", "density"],
    )
    late_home = move(g0, routes["late_home"])
    (g1,) = pairs(
        [("late", "a1", "a2", "g1", "", ""), ("late", "a1", "p3", "g1", "", "")],
        {"own": own, "late2": late2, "late_p3": late_p3},
        {"g1": tied(g1, g0)},
        ["g1"],
    )
    early_p3 = tied(early_p3, g1)
    g0, density = pairs(
        [("early", "a0", "p3", "g0", "", "lower")],
        {"early0": early0, "early_p3": early_p3},
        {"g0": g0, "density": density},
        ["g0", "density"],
        fresh=("g0",),
    )
    early_home = move(g0, routes["early_home"])
    late3 = move(tied(early_p3, g0), routes["to_late"])
    density = pl.pallas_call(
        count_kernel, out_shape=square, compiler_params=params, cost_estimate=cost, name="count"
    )(density)

    def meanwhile(earlier):
        (grad,) = pairs(
            [("early", "a1", "p3", "g1", "", "")], {"own": own, "early_p3": early_p3}, {"g1": tied(g1, earlier)}, ["g1"]
        )
        grad = pl.pallas_call(
            functools.partial(home_sum_kernel, nocc),
            out_shape=slab,
            in_specs=[SMEM, SMEM, ANY, ANY, ANY],
            out_specs=ANY,
            scratch_shapes=[
                pltpu.VMEM((2, rows, width), jnp.float32),
                pltpu.SemaphoreType.DMA((PIECES,)),
                pltpu.SemaphoreType.DMA((PIECES,)),
                pltpu.SemaphoreType.DMA((PIECES,)),
            ],
            input_output_aliases={2: 0},
            compiler_params=params,
            cost_estimate=cost,
            name="home_sum",
        )(occ_energy, pair_mask, grad, late_home, early_home)
        return pairs([("late", "a1", "a3", "g1", "", "")], {"own": own, "late3": late3}, {"g1": grad}, ["g1"])[0]

    blocks, gradient = reduced(density, nocc, ngrp, meanwhile, late_home)
    return gradient[None], blocks / (nocc * ngrp)


def combined(parts):
    while len(parts) > 1:
        parts = [x + y for x, y in zip(parts[::2], parts[1::2])]
    return parts[0]


def reduced(density, nocc, ngrp, meanwhile, arriving):
    place = lax.axis_index("occ")
    width = density.shape[1]
    rows = density.shape[0] // nocc
    blocks = density
    bit, radix = 1, 2
    while bit < nocc:
        radix = min(radix, nocc // bit)
        blocks = blocks.reshape(-1, radix, rows, width)
        digit = (place // bit) % radix
        received = []
        for j in range(radix):
            part = lax.dynamic_index_in_dim(blocks, digit ^ j, 1, keepdims=False)
            if j:
                part = lax.ppermute(part, "occ", [(o, o ^ (j * bit)) for o in range(nocc)])
            received.append(part)
        blocks = combined(received)
        bit, radix = bit * radix, 4
    blocks = tied(blocks.reshape(rows, width), arriving)
    others = [lax.ppermute(blocks, "grp", [(g, g ^ j) for g in range(ngrp)]) for j in range(1, ngrp)]
    made = meanwhile(blocks)
    others = lax.optimization_barrier((*others, made))[:-1]
    return combined([blocks, *others]), made


def solution(mesh):
    nocc = mesh.shape["occ"]
    if mesh.shape["grp"] != 4 or nocc < 4 or nocc & (nocc - 1):
        raise NotImplementedError("another mesh")
    placed = (P(AXES, None, None), P(), P(), P())
    return jax.shard_map(
        body,
        mesh=mesh,
        in_specs=placed,
        out_specs=(P(AXES, None, None), P("occ", None)),
        check_vma=False,
    )
```

```python
import functools

import jax
import jax.numpy as jnp
from jax import lax
from jax.experimental import pallas as pl
from jax.experimental.pallas import tpu as pltpu
from jax.sharding import PartitionSpec as P

AXES = ("occ", "grp")
PIECES = 4
VMEM_LIMIT = 63 * 1024 * 1024

SMEM = pl.BlockSpec(memory_space=pltpu.SMEM)
VMEM = pl.BlockSpec(memory_space=pltpu.VMEM)
ANY = pl.BlockSpec(memory_space=pl.ANY)


def plan(nocc):
    names = ("early2", "late0", "early0", "late2", "early_p3", "to_early", "to_late", "early_home", "late_home", "before")
    routes = {name: [] for name in names}

    def both(name, source, target):
        routes[name].append(tuple(4 * block + place for block, place in (source, target)))
        routes[name].append(tuple(4 * (nocc - 1 - block) + 3 - place for block, place in (source, target)))

    for even in range(0, nocc, 2):
        odd = even + 1
        both("early2", (odd, 2), (odd, 1))
        both("late0", (even, 0), (even, 1))
        both("early0", (odd, 0), (odd, 1))
        both("late2", (even, 2), (even, 1))
        both("early_p3", (even, 3), (odd, 1))
        both("to_early", (even, 1), (odd, 1))
        both("to_late", (odd, 1), (even, 1))
        both("early_home", (odd, 1), (odd, 0))
        both("late_home", (even, 1), (even, 0))
        if even:
            both("before", (even - 1, 1), (even, 1))
    return routes


def move(block, route):
    return lax.ppermute(block, AXES, route)


def tied(x, *earlier):
    return lax.optimization_barrier((x, *earlier))[0]


class Place:
    def __init__(self, nocc, energy_ref, mask_ref):
        occ, grp = lax.axis_index("occ"), lax.axis_index("grp")
        self.energy_ref, self.mask_ref = energy_ref, mask_ref
        self.last = nocc * 4 - 1
        self.own = occ * 4 + grp
        self.lower = grp <= 1
        hub = (grp == 1) | (grp == 2)
        inner = (lax.rem(occ, 2) == 1) == self.lower
        self.early, self.late = hub & inner, hub & ~inner
        self.from_late, self.from_early = ~hub & ~inner, ~hub & inner
        step = jnp.where(self.lower, 1, -1)
        a0 = occ * 4 + jnp.where(self.lower, 0, 3)
        self.index = {"a0": a0, "a1": a0 + step, "a2": a0 + 2 * step, "a3": a0 + 3 * step, "p3": a0 - step, "p2": a0 - 2 * step}

    def pair(self, x, y):
        offset = {"a0a1": 1, "a0a2": 2, "a1a2": 1, "a1a3": 2, "a0p2": 2, "a0p3": 1, "a1p3": 2}[x + y]
        i, j = self.index[x], self.index[y]
        there = (j >= 0) & (j <= self.last)
        i, j = jnp.clip(i, 0, self.last), jnp.clip(j, 0, self.last)
        active = there & (self.mask_ref[jnp.minimum(i, j), offset - 1] == 1)
        return active, self.energy_ref[i] + self.energy_ref[j]


ROWS = ((1,), (1,))
PLAIN = ((1,), (0,))
COLUMNS = ((0,), (0,))


def mul(left, right, dims):
    return lax.dot_general(left, right, (dims, ((), ())), preferred_element_type=jnp.float32)


def halves(x):
    high = x.astype(jnp.bfloat16)
    return high, (x - high.astype(jnp.float32)).astype(jnp.bfloat16)


def parts(x, other, axis):
    high, low = halves(x)
    return jnp.concatenate([high, low, high] if other else [high, high, low], axis)


def half_squares(t):
    high, low = halves(t)
    left, right = [high, high], [high * 0.5, low]
    return mul(jnp.concatenate(left, 1), jnp.concatenate(right, 1), ROWS) + mul(
        jnp.concatenate(left, 0), jnp.concatenate(right, 0), COLUMNS
    )


def home_kernel(nocc, energy_ref, mask_ref, vir_ref, slab_ref, grad_ref, density_ref, levels_ref):
    rows = slab_ref.shape[0]
    spread = jnp.broadcast_to(vir_ref[...], (rows, rows))
    levels_ref[...] = spread + spread.T
    energy = energy_ref[Place(nocc, energy_ref, mask_ref).own]
    slab = slab_ref[...]
    t = mul(parts(slab, False, 1), parts(slab, True, 1), ROWS) / (2.0 * energy - levels_ref[...])
    t3 = parts(t, False, 1)
    grad_ref[...] = 2.0 * mul(t3, parts(slab, True, 0), PLAIN)
    density_ref[...] = mul(t3, parts(t, True, 1), ROWS)


def slots_of(tasks):
    found = {}
    for role, x, y, *_ in tasks:
        for orbital in (x, y):
            name = "own" if orbital == "a1" else role + orbital[1:] if orbital[0] == "a" else role + "_" + orbital
            if name not in found.setdefault(role, {}):
                found[role][name] = (len(found[role]), orbital)
    return found


def pairs_kernel(nocc, tasks, names, given, made, fresh, energy_ref, mask_ref, levels_ref, *refs):
    slabs, refs = dict(zip(names, refs[:len(names)])), refs[len(names):]
    before, refs = dict(zip(given, refs[:len(given)])), refs[len(given):]
    after, refs = dict(zip(made, refs[:len(made)])), refs[len(made):]
    slots, split, slabs_sem, sums, square, levels, t_ref, sums_sem, meta, energies, state = refs
    width = slots.shape[2]
    place = Place(nocc, energy_ref, mask_ref)
    roles = {"early": place.early, "late": place.late}
    layout = slots_of(tasks)
    added = {name: jnp.bool_(False) for name in ("g0", "g1", "density")}
    needed = {role: [jnp.bool_(False)] * len(layout[role]) for role in layout}
    for k, (role, x, y, left, right, counted) in enumerate(tasks):
        active, energy = place.pair(x, y)
        active = active & roles[role]
        energies[k] = energy
        meta[k, 0] = active.astype(jnp.int32)
        for column, orbital in ((1, x), (2, y)):
            slot = next(slot for slot, held in layout[role].values() if held == orbital)
            meta[k, column] = slot
            needed[role][slot] = needed[role][slot] | active
        meta[k, 3] = ("", "g0", "g1").index(left)
        meta[k, 4] = ("", "g0", "g1").index(right)
        counts = place.lower if counted == "lower" else jnp.bool_(bool(counted))
        for name, used in ((left, active), (right, active), ("density", active & counts)):
            if name:
                added[name] = added[name] | used
        meta[k, 5] = counts.astype(jnp.int32)
    run = functools.reduce(jnp.logical_or, [roles[role] for role in layout])
    held = {"g0": sums.at[0], "g1": sums.at[1], "density": square}
    uses = {name: run if name in fresh or name not in given else added[name] for name in made}

    def wanted(name, copies):
        @pl.when(uses[name])
        def _():
            copies(name)

    @pl.when(run)
    def _():
        state[0] = 0
        for s in range(slots.shape[0]):
            meta[s, 6] = 0
        for role in layout:
            for name, (s, _) in layout[role].items():

                @pl.when(needed[role][s])
                def _():
                    meta[s, 6] = 1
                    pltpu.make_async_copy(slabs[name], slots.at[s], slabs_sem.at[s]).start()

        pltpu.make_async_copy(levels_ref, levels, sums_sem.at[0]).start()
        for q, name in enumerate(given):
            wanted(name, lambda name: pltpu.make_async_copy(before[name], held[name], sums_sem.at[q + 1]).start())
        if "g0" in made and "g0" not in given:
            sums[0] = jnp.zeros(sums.shape[1:], sums.dtype)

        def arrived():
            @pl.when(state[0] == 0)
            def _():
                pltpu.make_async_copy(levels_ref, levels, sums_sem.at[0]).wait()
                for q, name in enumerate(given):
                    wanted(name, lambda name: pltpu.make_async_copy(before[name], held[name], sums_sem.at[q + 1]).wait())
                state[0] = 1

        @pl.loop(0, len(tasks))
        def _(k):
            @pl.when(meta[k, 0] == 1)
            def _():
                @pl.loop(1, 3)
                def _(column):
                    s = meta[k, column]

                    @pl.when(meta[s, 6] == 1)
                    def _():
                        pltpu.make_async_copy(slabs[names[0]], slots.at[s], slabs_sem.at[s]).wait()
                        high, low = halves(slots[s])
                        split[s, :, 0:width] = high
                        split[s, :, width:2 * width] = low
                        split[s, :, 2 * width:3 * width] = high
                        meta[s, 6] = 0

                x, y = split.at[meta[k, 1]], split.at[meta[k, 2]]
                t_ref[...] = mul(x[:, width:], y[:, :2 * width], ROWS) + mul(x[:, :width], y[:, :width], ROWS)
                arrived()
                t = t_ref[...] / (energies[k] - levels[...])
                t_ref[...] = t
                high, low = halves(t)

                def onto(target, z, dims):
                    wide = mul(high, z[:, :2 * width], dims)
                    sums[target] += wide[:, :width] + wide[:, width:] + mul(low, z[:, :width], dims)

                if any(task[3] for task in tasks):

                    @pl.when(meta[k, 3] > 0)
                    def _():
                        onto(meta[k, 3] - 1, y, PLAIN)

                if any(task[4] for task in tasks):

                    @pl.when(meta[k, 4] > 0)
                    def _():
                        onto(meta[k, 4] - 1, x, COLUMNS)

                if any(task[5] for task in tasks):

                    @pl.when(meta[k, 5] == 1)
                    def _():
                        square[...] += half_squares(t_ref[...])

        arrived()
        for q, name in enumerate(made):
            wanted(name, lambda name: pltpu.make_async_copy(held[name], after[name], sums_sem.at[q]).start())
        for q, name in enumerate(made):
            wanted(name, lambda name: pltpu.make_async_copy(held[name], after[name], sums_sem.at[q]).wait())


def count_kernel(density_ref, out_ref):
    total = density_ref[...]
    out_ref[...] = total + total.T


def home_sum_kernel(nocc, energy_ref, mask_ref, own_ref, late_ref, early_ref, out_ref, slots, own_sem, sum_sem, out_sem):
    place = Place(nocc, energy_ref, mask_ref)
    step = own_ref.shape[0] // PIECES

    def add(source):
        pieces = [pl.ds(p * step, step) for p in range(PIECES)]

        def own(p):
            return pltpu.make_async_copy(own_ref.at[pieces[p]], slots.at[0, pieces[p]], own_sem.at[p])

        def other(p):
            return pltpu.make_async_copy(source.at[pieces[p]], slots.at[1, pieces[p]], sum_sem.at[p])

        def out(p):
            return pltpu.make_async_copy(slots.at[0, pieces[p]], out_ref.at[pieces[p]], out_sem.at[p])

        for p in range(PIECES):
            own(p).start()
            other(p).start()
        for p in range(PIECES):
            own(p).wait()
            other(p).wait()
            slots[0, pieces[p]] += slots[1, pieces[p]]
            out(p).start()
        for p in range(PIECES):
            out(p).wait()

    @pl.when(place.from_late)
    def _():
        add(late_ref)

    @pl.when(place.from_early)
    def _():
        add(early_ref)


def body(slabs, occ_energy, vir_energy, pair_mask):
    nocc, ngrp = lax.axis_size("occ"), lax.axis_size("grp")
    routes = plan(nocc)
    own = slabs[0]
    rows, width = own.shape
    slab = jax.ShapeDtypeStruct((rows, width), jnp.float32)
    square = jax.ShapeDtypeStruct((rows, rows), jnp.float32)
    shapes = {"g0": slab, "g1": slab, "density": square}
    cost = pl.CostEstimate(flops=1000, bytes_accessed=1000, transcendentals=0)
    params = pltpu.CompilerParams(vmem_limit_bytes=VMEM_LIMIT)

    def pairs(tasks, there, given, made, fresh=()):
        inputs = [levels, *there.values(), *given.values()]
        first = 2 + len(inputs) - len(given)
        count = max(len(held) for held in slots_of(tasks).values())
        return pl.pallas_call(
            functools.partial(pairs_kernel, nocc, tasks, list(there), list(given), made, fresh),
            out_shape=[shapes[name] for name in made],
            in_specs=[SMEM, SMEM] + [ANY] * len(inputs),
            out_specs=[ANY] * len(made),
            scratch_shapes=[
                pltpu.VMEM((count, rows, width), jnp.float32),
                pltpu.VMEM((count, rows, 3 * width), jnp.bfloat16),
                pltpu.SemaphoreType.DMA((count,)),
                pltpu.VMEM((2, rows, width), jnp.float32),
                pltpu.VMEM((rows, rows), jnp.float32),
                pltpu.VMEM((rows, rows), jnp.float32),
                pltpu.VMEM((rows, rows), jnp.float32),
                pltpu.SemaphoreType.DMA((4,)),
                pltpu.SMEM((max(len(tasks), count), 8), jnp.int32),
                pltpu.SMEM((len(tasks),), jnp.float32),
                pltpu.SMEM((1,), jnp.int32),
            ],
            input_output_aliases={first + q: made.index(n) for q, n in enumerate(given) if n not in fresh},
            compiler_params=params,
            cost_estimate=cost,
            name="pairs",
        )(occ_energy, pair_mask, *inputs)

    early2 = move(own, routes["early2"])
    late0 = move(own, routes["late0"])
    home_grad, home_density, levels = pl.pallas_call(
        functools.partial(home_kernel, nocc),
        out_shape=[slab, square, square],
        in_specs=[SMEM, SMEM, VMEM, VMEM],
        out_specs=[VMEM] * 3,
        compiler_params=params,
        cost_estimate=cost,
        name="home_pair",
    )(occ_energy, pair_mask, vir_energy.reshape(1, rows), own)
    late0 = tied(late0, home_density)
    early3 = move(late0, routes["early2"])
    early0 = move(tied(own, late0), routes["early0"])
    late_p2 = move(tied(early2, home_density), routes["before"])
    g0, g1, density = pairs(
        [("early", "a1", "a2", "g1", "", "all"), ("late", "a0", "a1", "g0", "g1", "all")],
        {"own": own, "early2": early2, "late0": late0},
        {"g1": home_grad, "density": home_density},
        ["g0", "g1", "density"],
    )
    early3 = tied(early3, g1)
    late2 = move(tied(own, early3), routes["late2"])
    late_p3 = move(early3, routes["before"])
    g0, g1, density = pairs(
        [
            ("early", "a1", "a3", "g1", "", "all"),
            ("early", "a0", "a1", "g0", "g1", "all"),
            ("late", "a0", "p2", "g0", "", "all"),
        ],
        {"own": own, "early0": early0, "early3": early3, "late0": late0, "late_p2": late_p2},
        {"g0": g0, "g1": g1, "density": density},
        ["g0", "g1", "density"],
    )
    early_p3 = move(tied(own, g1), routes["early_p3"])
    late2 = tied(late2, g1)
    early_p2 = move(late2, routes["to_early"])
    g0, density = pairs(
        [
            ("early", "a0", "a2", "g0", "", "all"),
            ("early", "a0", "p2", "g0", "", "all"),
            ("late", "a0", "a2", "g0", "", ""),
            ("late", "a0", "p3", "g0", "", ""),
        ],
        {
            "early0": early0, "early2": early2, "early_p2": early_p2, "late0": late0, "late2": late2,
            "late_p3": tied(late_p3, g1),
        },
        {"g0": g0, "density": density},
        ["g0", "density"],
    )
    late_home = move(g0, routes["late_home"])
    g1, density = pairs(
        [
            ("late", "a1", "a2", "g1", "", ""),
            ("late", "a1", "p3", "g1", "", ""),
            ("late", "a0", "p3", "", "", "lower"),
        ],
        {"own": own, "late0": late0, "late2": late2, "late_p3": late_p3},
        {"g1": tied(g1, g0), "density": density},
        ["g1", "density"],
    )
    early_p3 = tied(early_p3, g1)
    g0, density = pairs(
        [("early", "a0", "p3", "g0", "", "lower")],
        {"early0": early0, "early_p3": early_p3},
        {"g0": g0, "density": density},
        ["g0", "density"],
        fresh=("g0",),
    )
    early_home = move(g0, routes["early_home"])
    late3 = move(tied(early_p3, g0), routes["to_late"])
    density = pl.pallas_call(
        count_kernel, out_shape=square, compiler_params=params, cost_estimate=cost, name="count"
    )(density)

    def meanwhile(earlier):
        (grad,) = pairs(
            [("early", "a1", "p3", "g1", "", "")], {"own": own, "early_p3": early_p3}, {"g1": tied(g1, earlier)}, ["g1"]
        )
        grad = pl.pallas_call(
            functools.partial(home_sum_kernel, nocc),
            out_shape=slab,
            in_specs=[SMEM, SMEM, ANY, ANY, ANY],
            out_specs=ANY,
            scratch_shapes=[
                pltpu.VMEM((2, rows, width), jnp.float32),
                pltpu.SemaphoreType.DMA((PIECES,)),
                pltpu.SemaphoreType.DMA((PIECES,)),
                pltpu.SemaphoreType.DMA((PIECES,)),
            ],
            input_output_aliases={2: 0},
            compiler_params=params,
            cost_estimate=cost,
            name="home_sum",
        )(occ_energy, pair_mask, grad, late_home, early_home)
        return pairs([("late", "a1", "a3", "g1", "", "")], {"own": own, "late3": late3}, {"g1": grad}, ["g1"])[0]

    blocks, gradient = reduced(density, nocc, ngrp, meanwhile, late_home)
    return gradient[None], blocks / (nocc * ngrp)


def combined(parts):
    while len(parts) > 1:
        parts = [x + y for x, y in zip(parts[::2], parts[1::2])]
    return parts[0]


def reduced(density, nocc, ngrp, meanwhile, arriving):
    place = lax.axis_index("occ")
    width = density.shape[1]
    rows = density.shape[0] // nocc
    blocks = density
    bit, radix = 1, 2
    while bit < nocc:
        radix = min(radix, nocc // bit)
        blocks = blocks.reshape(-1, radix, rows, width)
        digit = (place // bit) % radix
        received = []
        for j in range(radix):
            part = lax.dynamic_index_in_dim(blocks, digit ^ j, 1, keepdims=False)
            if j:
                part = lax.ppermute(part, "occ", [(o, o ^ (j * bit)) for o in range(nocc)])
            received.append(part)
        blocks = combined(received)
        bit, radix = bit * radix, 4
    blocks = tied(blocks.reshape(rows, width), arriving)
    others = [lax.ppermute(blocks, "grp", [(g, g ^ j) for g in range(ngrp)]) for j in range(1, ngrp)]
    made = meanwhile(blocks)
    others = lax.optimization_barrier((*others, made))[:-1]
    return combined([blocks, *others]), made


def solution(mesh):
    nocc = mesh.shape["occ"]
    if mesh.shape["grp"] != 4 or nocc < 4 or nocc & (nocc - 1):
        raise NotImplementedError("another mesh")
    placed = (P(AXES, None, None), P(), P(), P())
    return jax.shard_map(
        body,
        mesh=mesh,
        in_specs=placed,
        out_specs=(P(AXES, None, None), P("occ", None)),
        check_vma=False,
    )
```
